256 devices in a mesh: dp: 32 (over y, x, core), mp: 8 (over z).
Axes of the slice: x: 4, y: 4, z: 8, core: 2. Of those that a mesh axis runs over, the one named last changes fastest.
Arguments:
- tokens: bfloat16 [32768, 2048], P(('dp', 'mp')), may hold values from -6 to 6
- out_grad: bfloat16 [32768, 7168], P('dp', 'mp'), may hold values from -0.1875 to 0.1875
- error: bfloat16 [32, 2048, 7168], P('dp', None, 'mp'), may hold values from -6 to 6
- q_prev: float32 [8, 7168], P(None, 'mp'), may hold values from -6 to 6
Outputs:
- p_factor: float32 [8, 2048], replicated
- q_factor: float32 [8, 7168], P(None, 'mp')
- new_error: bfloat16 [32, 2048, 7168], P('dp', None, 'mp')
The draws below stay inside these ranges and needn't reach their ends.
All inputs are finite; a program needn't handle non-finite values.
Results may differ from the reference program's by a relative error of at most 0.0004.
Values may be sent and summed in bfloat16 or wider, within the bound.
No kernel may reach another device: no remote copies, remote signals or barrier semaphores. Data moves between devices by JAX's collectives and lax.ppermute only.
A program may use at most 64 MiB of HBM per device.

```python
import jax
import jax.numpy as jnp
from jax import lax

D = 2048
FF = 7168
R = 8
TOK_DEV = 1024
TOKENS = 32768
N_DP = 32


def level_of(key, dims, shards, low, largest):
    level, own = 1.0, jax.random.fold_in(key, 6)
    for dim, blocks in shards:
        heights = jnp.exp(jax.random.uniform(jax.random.fold_in(own, dim), (blocks,), jnp.float32, low / len(shards), largest / len(shards)))
        level = level * jnp.repeat(heights, dims[dim] // blocks).reshape([-1 if axis == dim else 1 for axis in range(len(dims))])
    return level


def scatter_about(own_key, shape, spread, bound, cuts=(), dtype=jnp.bfloat16):
    values = spread * jax.random.normal(own_key, shape, jnp.float32)
    if cuts:
        values = values * level_of(own_key, shape, cuts, -0.22, 0.18)
    return jnp.clip(values, -bound, bound).astype(dtype)


def setup_inputs(seed: int = 0) -> dict:
    arg_keys = jax.random.split(jax.random.key(seed), 5)
    tokens = scatter_about(arg_keys[0], (TOKENS, D), 1.0, 6.0, ((0, 256),))
    out_grad = scatter_about(arg_keys[1], (TOKENS, FF), TOK_DEV ** -0.5, 0.1875, ((0, 32), (1, 8)))
    error = scatter_about(arg_keys[2], (N_DP, D, FF), 1.0, 6.0, ((0, 32), (2, 8)))
    q_prev = scatter_about(arg_keys[3], (R, FF), 1.0, 6.0, ((1, 8),), jnp.float32)
    return dict(tokens=tokens, out_grad=out_grad, error=error, q_prev=q_prev)


def orthonormal(rows):
    done = []
    for index in range(rows.shape[0]):
        vector = rows[index]
        for earlier in done:
            vector = vector - jnp.sum(vector * earlier) * earlier
        vector = vector / jnp.sqrt(jnp.sum(vector * vector) + 1e-06)
        done.append(vector)
    return jnp.stack(done)

def reference(tokens, out_grad, error, q_prev):
    high = lax.Precision.HIGHEST
    inputs = tokens.astype(jnp.float32).reshape(N_DP, TOK_DEV, D)
    grads = out_grad.astype(jnp.float32).reshape(N_DP, TOK_DEV, FF)

    def left_step(total, items):
        x_rows, g_rows, err = items
        reduced = jnp.dot(g_rows, q_prev.T, precision=high)
        term = jnp.dot(reduced.T, x_rows, precision=high)
        term = term + jnp.dot(q_prev, err.astype(jnp.float32).T, precision=high)
        return (total + term, None)
    p_sum, _ = lax.scan(left_step, jnp.zeros((R, D), jnp.float32), (inputs, grads, error))
    p_factor = orthonormal(p_sum)

    def right_step(total, items):
        x_rows, g_rows, err = items
        projected = jnp.dot(p_factor, x_rows.T, precision=high)
        term = jnp.dot(projected, g_rows, precision=high)
        term = term + jnp.dot(p_factor, err.astype(jnp.float32), precision=high)
        return (total + term, None)
    q_total, _ = lax.scan(right_step, jnp.zeros((R, FF), jnp.float32), (inputs, grads, error))
    q_factor = q_total / N_DP

    def residue(items):
        x_rows, g_rows, err = items
        merged = jnp.dot(x_rows.T, g_rows, precision=high) + err.astype(jnp.float32)
        return (merged - jnp.dot(p_factor.T, q_factor, precision=high)).astype(jnp.bfloat16)
    new_error = lax.map(residue, (inputs, grads, error))
    return (p_factor, q_factor, new_error)
```

```python
import functools

import jax
import jax.numpy as jnp
from jax import lax
from jax.experimental import pallas as pl
from jax.experimental.pallas import tpu as pltpu
from jax.sharding import PartitionSpec as P

MP = 8
DP = 32
R = 8


def shift(size, step):
    return [(i, (i + step) % size) for i in range(size)]


CORES = [(i, i ^ 1) for i in range(DP)]
CHIPS = [[2 * i for i in range(DP // 2)], [2 * i + 1 for i in range(DP // 2)]]


def split3(x):
    first = lax.reduce_precision(x, 8, 7)
    rest = x - first
    second = lax.reduce_precision(rest, 8, 7)
    third = rest - second
    return jnp.concatenate([first, second, third], axis=0).astype(jnp.bfloat16)


def fold3(x):
    rows = x.shape[0] // 3
    return (x[2 * rows :] + x[rows : 2 * rows]) + x[:rows]


def dot(a, b, contract):
    return lax.dot_general(a, b, (contract, ((), ())), preferred_element_type=jnp.float32)


def gram_schmidt_kernel(rows_ref, out_ref):
    rows = rows_ref[...]
    index = lax.broadcasted_iota(jnp.int32, (R, 1), 0)
    for i in range(R):
        vector = rows[i : i + 1]
        norm = jnp.sqrt(jnp.sum(vector * vector, axis=1, keepdims=True) + 1e-06)
        vector = vector / norm
        products = jnp.sum(rows * vector, axis=1, keepdims=True)
        rows = jnp.where(index > i, rows - products * vector, jnp.where(index == i, vector, rows))
    out_ref[...] = rows


def gram_schmidt(rows):
    return pl.pallas_call(
        gram_schmidt_kernel,
        out_shape=jax.ShapeDtypeStruct(rows.shape, rows.dtype),
        in_specs=[pl.BlockSpec(memory_space=pltpu.VMEM)],
        out_specs=pl.BlockSpec(memory_space=pltpu.VMEM),
    )(rows)


def spread(x, axis, size, groups=None):
    wide = jnp.broadcast_to(x[None], (size,) + x.shape)
    return lax.all_to_all(wide, axis, 0, 0, axis_index_groups=groups)


def on_device(tokens, out_grad, error, q_prev):
    err = error[0]
    me = lax.axis_index("mp")
    core = lax.axis_index("dp") % 2
    half = tokens.shape[0] // 2
    rows = tokens.shape[0]

    blocks, order = [tokens], [me]
    right = left = tokens
    for step in range(1, 4):
        right = lax.ppermute(right, "mp", shift(MP, 1))
        left = lax.ppermute(left, "mp", shift(MP, -1))
        blocks += [right, left]
        order += [(me - step) % MP, (me + step) % MP]
    top = lax.ppermute(right[:half], "mp", shift(MP, 1))
    bottom = lax.ppermute(left[half:], "mp", shift(MP, -1))
    blocks += [top, bottom]
    order += [(me + 4) % MP]
    gathered = jnp.concatenate(blocks, axis=0)
    grads = jnp.concatenate([lax.dynamic_slice_in_dim(out_grad, o * rows, rows, 0) for o in order], axis=0)

    q_terms = split3(q_prev)
    reduced = fold3(dot(q_terms, out_grad, ((1,), (1,))))
    reduced = reduced.reshape(R, MP, rows).transpose(1, 0, 2)
    reduced = jnp.sum(lax.all_to_all(reduced, "mp", 0, 0), axis=0)
    part = fold3(dot(split3(reduced), tokens, ((1,), (0,)))) + fold3(dot(q_terms, err, ((1,), (1,))))
    width = part.shape[1] // MP
    part = part.reshape(R, MP, width).transpose(1, 0, 2)
    part = jnp.sum(lax.all_to_all(part, "mp", 0, 0), axis=0)
    part = jnp.sum(spread(part, "dp", DP), axis=0)
    p_sum = spread(part, "mp", MP).transpose(1, 0, 2).reshape(R, MP * width)
    p_factor = gram_schmidt(p_sum)

    p_terms = split3(p_factor)
    projected = fold3(dot(p_terms, gathered, ((1,), (1,))))
    q_local = fold3(dot(split3(projected), grads, ((1,), (0,)))) + fold3(dot(p_terms, err, ((1,), (0,))))
    columns = q_local.shape[1]
    wide = jnp.pad(q_local, ((0, 0), (0, 1024 - columns))).reshape(R, 2, 512).transpose(1, 0, 2)
    keep = lax.dynamic_index_in_dim(wide, core, 0, False)
    send = lax.dynamic_index_in_dim(wide, 1 - core, 0, False)
    mine = keep + lax.ppermute(send, "dp", CORES)
    mine = jnp.sum(spread(mine, "dp", DP // 2, CHIPS), axis=0) / DP
    other = lax.ppermute(mine, "dp", CORES)
    first = jnp.where(core == 0, mine, other)
    second = jnp.where(core == 0, other, mine)
    q_factor = jnp.concatenate([first, second], axis=1)[:, :columns]

    grad = dot(gathered, grads, ((0,), (0,)))
    q_terms = split3(q_factor)
    left_terms = jnp.concatenate([p_terms[:8], p_terms[:8], p_terms[:8], p_terms[8:16], p_terms[8:16], p_terms[16:]], axis=0)
    right_terms = jnp.concatenate([q_terms, q_terms[:16], q_terms[:8]], axis=0)
    new_error = (grad + err.astype(jnp.float32) - dot(left_terms, right_terms, ((0,), (0,)))).astype(jnp.bfloat16)
    return (p_factor, q_factor, new_error[None])


def solution(mesh):
    placed = (P(("dp", "mp"), None), P("dp", "mp"), P("dp", None, "mp"), P(None, "mp"))
    return jax.shard_map(
        on_device,
        mesh=mesh,
        in_specs=placed,
        out_specs=(P(), P(None, "mp"), P("dp", None, "mp")),
        check_vma=False,
    )
```

```python
import jax
import jax.numpy as jnp
from jax import lax
from jax.experimental import pallas as pl
from jax.experimental.pallas import tpu as pltpu
from jax.sharding import PartitionSpec as P

MP = 8
DP = 32
R = 8
HALF = 512
TOKENS = 1024
F32 = jnp.float32
BF16 = jnp.bfloat16
VMEM = pltpu.MemorySpace.VMEM


def shift(size, step):
    return [(i, (i + step) % size) for i in range(size)]


CORES = [(i, i ^ 1) for i in range(DP)]
CHIPS = [[2 * i for i in range(DP // 2)], [2 * i + 1 for i in range(DP // 2)]]


def after(x, *others):
    return lax.optimization_barrier((x,) + others)[0]


def terms(x):
    first = x.astype(BF16).astype(F32)
    rest = x - first
    second = rest.astype(BF16).astype(F32)
    return first, second, rest - second


def split3(x):
    return jnp.concatenate(terms(x), axis=0).astype(BF16)


def fold3(x):
    rows = x.shape[0] // 3
    return (x[2 * rows :] + x[rows : 2 * rows]) + x[:rows]


def dot(a, b, left, right):
    return lax.dot_general(a, b, (((left,), (right,)), ((), ())), preferred_element_type=F32)


def local(kernel, out, *args, spaces=None, mib=8, scratch=(), **kw):
    spaces = spaces or [VMEM] * len(args)
    return pl.pallas_call(
        kernel,
        out_shape=out,
        in_specs=[pl.BlockSpec(memory_space=s) for s in spaces],
        out_specs=jax.tree.map(lambda _: pl.BlockSpec(memory_space=VMEM), out),
        scratch_shapes=scratch,
        compiler_params=pltpu.CompilerParams(vmem_limit_bytes=mib << 20),
        **kw,
    )(*args)


def shape(*dims, dtype=F32):
    return jax.ShapeDtypeStruct(dims, dtype)


def pieces(size, count):
    step = size // count
    return [slice(i * step, (i + 1) * step) for i in range(count)]


def far(x):
    return pltpu.with_memory_space_constraint(x, pltpu.MemorySpace.HBM)


def reduce_kernel(q_ref, g_ref, out_ref, q_held, held, sems):
    first = pltpu.make_async_copy(q_ref, q_held, sems.at[0])
    first.start()
    copies = [pltpu.make_async_copy(g_ref.at[at], held.at[at], sems.at[1 + i]) for i, at in enumerate(pieces(TOKENS, 4))]
    for copy in copies:
        copy.start()
    first.wait()
    q = split3(q_held[...])
    for i, (copy, at) in enumerate(zip(copies, pieces(TOKENS, 4))):
        copy.wait()
        value = fold3(dot(q, held[at], 1, 1))
        out_ref[2 * i] = value[:, :128]
        out_ref[2 * i + 1] = value[:, 128:]


def error_left_kernel(q_ref, err_ref, out_ref, q_held, held, sems):
    depth = err_ref.shape[0]
    first = pltpu.make_async_copy(q_ref, q_held, sems.at[0])
    first.start()
    copies = [pltpu.make_async_copy(err_ref.at[at], held.at[at], sems.at[1 + i]) for i, at in enumerate(pieces(depth, 4))]
    for copy in copies:
        copy.start()
    first.wait()
    q = split3(q_held[...])
    for copy, at in zip(copies, pieces(depth, 4)):
        copy.wait()
        out_ref[:, at] = fold3(dot(q, held[at], 1, 1))


def left_kernel(parts_ref, x_ref, more_ref, out_ref):
    reduced = jnp.sum(parts_ref[...], axis=0)
    value = fold3(dot(split3(reduced), x_ref[...], 1, 0)) + more_ref[...]
    for z in range(MP):
        out_ref[z] = value[:, z * 256 : (z + 1) * 256]


def sum_spread_kernel(parts_ref, out_ref):
    value = jnp.sum(parts_ref[...], axis=0)
    out_ref[...] = jnp.broadcast_to(value[None], out_ref.shape)


def gram_schmidt_kernel(parts_ref, out_ref):
    rows = jnp.concatenate([parts_ref[z] for z in range(MP)], axis=1)
    index = lax.broadcasted_iota(jnp.int32, (R, 1), 0)
    for i in range(R):
        vector = rows[i : i + 1]
        products = jnp.sum(rows * vector, axis=1, keepdims=True)
        scale = 1.0 / jnp.sqrt(products[i : i + 1] + 1e-06)
        vector = vector * scale
        rows = jnp.where(index > i, rows - (products * scale) * vector, jnp.where(index == i, vector, rows))
    out_ref[...] = rows


def right_kernel(p_ref, err_ref, g_ref, *refs):
    blocks, (keep_ref, send_ref, rows_ref, grads_ref, held, sems) = refs[:9], refs[9:]
    me = lax.axis_index("mp")
    starts = [me * 128]
    for step in range(1, 4):
        starts += [lax.rem(me + MP - step, MP) * 128, lax.rem(me + step, MP) * 128]
    last = lax.rem(me + 4, MP) * 128
    starts += [last, last + 64]
    copies = [pltpu.make_async_copy(g_ref, grads_ref.at[pl.ds(0, TOKENS)], sems.at[9])]
    for i, (block, start) in enumerate(zip(blocks, starts)):
        size = block.shape[0]
        copies.append(pltpu.make_async_copy(block, rows_ref.at[pl.ds(pl.multiple_of(start, size), size)], sems.at[i]))
    copies.append(pltpu.make_async_copy(err_ref, held, sems.at[10]))
    for copy in copies[1:] + copies[:1]:
        copy.start()
    a, b, c = terms(p_ref[...])
    left = jnp.concatenate([a, b, c], axis=0).astype(BF16)
    rows_ref[TOKENS:] = jnp.concatenate([a, a, a, b, b, c, jnp.zeros((2 * R, a.shape[1]), F32)], axis=0).astype(BF16)
    grads_ref[TOKENS:] = jnp.zeros((8 * R, grads_ref.shape[1]), BF16)
    for copy in copies[1:10]:
        copy.wait()
    projected = fold3(dot(left, rows_ref[:TOKENS], 1, 1))
    copies[0].wait()
    value = fold3(dot(split3(projected), grads_ref[:TOKENS], 1, 0))
    copies[10].wait()
    value = value + fold3(dot(left, held[...], 1, 0))
    first = value[:, :HALF]
    second = jnp.concatenate([value[:, HALF:], jnp.zeros((R, 2 * HALF - value.shape[1]), F32)], axis=1)
    core = lax.rem(lax.axis_index("dp"), 2)
    keep_ref[...] = jnp.where(core == 0, first, second)
    send_ref[...] = jnp.where(core == 0, second, first)


def add_spread_kernel(a_ref, b_ref, out_ref):
    out_ref[...] = jnp.broadcast_to((a_ref[...] + b_ref[...])[None], out_ref.shape)


def mean_kernel(parts_ref, out_ref):
    out_ref[...] = jnp.sum(parts_ref[...], axis=0) / DP


def right_factor_kernel(mine_ref, other_ref, grads_ref, q_ref, out_ref):
    core = lax.rem(lax.axis_index("dp"), 2)
    mine, other = mine_ref[...], other_ref[...]
    first = jnp.where(core == 0, mine, other)
    second = jnp.where(core == 0, other, mine)
    q = jnp.concatenate([first, second[:, : q_ref.shape[1] - HALF]], axis=1)
    q_ref[...] = q
    a, b, c = terms(-q)
    out_ref[TOKENS:] = jnp.concatenate([a, b, c, a, b, a, jnp.zeros((2 * R, a.shape[1]), F32)], axis=0).astype(BF16)


def exchange(x, axis, groups=None):
    return lax.all_to_all(x, axis, 0, 0, axis_index_groups=groups)


def on_device(tokens, out_grad, error, q_prev):
    err = error[0]
    depth, columns = err.shape
    half = tokens.shape[0] // 2

    def pass_on(right, left):
        return lax.ppermute(right, "mp", shift(MP, 1)), lax.ppermute(left, "mp", shift(MP, -1))

    right1, left1 = pass_on(tokens, tokens)
    hbm = pltpu.MemorySpace.HBM
    dma = pltpu.SemaphoreType.DMA
    held = pltpu.VMEM((R, columns), F32)
    reduced = local(
        reduce_kernel, shape(MP, R, 128), far(q_prev), far(out_grad), spaces=[hbm, hbm], scratch=[held, pltpu.VMEM(out_grad.shape, BF16), dma((5,))]
    )
    more = local(
        error_left_kernel, shape(R, depth), far(q_prev), far(err), spaces=[hbm, hbm], scratch=[held, pltpu.VMEM(err.shape, BF16), dma((5,))]
    )
    reduced = exchange(reduced, "mp")
    part = local(left_kernel, shape(MP, R, 256), reduced, tokens, more)
    right2, left2 = pass_on(after(right1, part), after(left1, part))
    part = exchange(after(part, right1, left1), "mp")
    part = local(sum_spread_kernel, shape(DP, R, 256), part)
    right3, left3 = pass_on(after(right2, part), after(left2, part))
    part = exchange(after(part, right2, left2), "dp")
    part = local(sum_spread_kernel, shape(MP, R, 256), part)
    right4, left4 = pass_on(after(right3, part)[:half], after(left3, part)[half:])
    part = exchange(after(part, right3, left3), "mp")
    p_factor = local(gram_schmidt_kernel, pltpu.VMEM((R, depth), F32), part)
    blocks = (tokens, right1, left1, right2, left2, right3, left3, right4, left4)

    keep, send, rows, grads = local(
        right_kernel,
        (
            shape(R, HALF),
            shape(R, HALF),
            pltpu.VMEM((TOKENS + 8 * R, depth), BF16),
            pltpu.VMEM((TOKENS + 8 * R, columns), BF16),
        ),
        pltpu.with_memory_space_constraint(p_factor, VMEM),
        far(err),
        far(out_grad),
        *blocks,
        spaces=[VMEM, hbm, hbm] + [pl.ANY] * 9,
        scratch=[pltpu.VMEM(err.shape, BF16), dma((11,))],
    )
    wide = local(add_spread_kernel, shape(DP // 2, R, HALF), keep, lax.ppermute(send, "dp", CORES))
    mine = local(mean_kernel, shape(R, HALF), exchange(wide, "dp", CHIPS))
    other = lax.ppermute(mine, "dp", CORES)
    q_factor, grads = local(
        right_factor_kernel,
        (shape(R, columns), pltpu.VMEM(grads.shape, BF16)),
        mine,
        other,
        pltpu.with_memory_space_constraint(grads, VMEM),
        input_output_aliases={2: 1},
    )
    new_error = (dot(rows, grads, 0, 0) + err.astype(F32)).astype(BF16)
    return (p_factor, q_factor, new_error[None])


def solution(mesh):
    placed = (P(("dp", "mp"), None), P("dp", "mp"), P("dp", None, "mp"), P(None, "mp"))
    return jax.shard_map(
        on_device,
        mesh=mesh,
        in_specs=placed,
        out_specs=(P(), P(None, "mp"), P("dp", None, "mp")),
        check_vma=False,
    )
```

```python
import functools

import jax
import jax.numpy as jnp
from jax import lax
from jax.experimental import pallas as pl
from jax.experimental.pallas import tpu as pltpu
from jax.sharding import PartitionSpec as P

MP = 8
DP = 32
R = 8
HALF = 512
TOKENS = 1024
CHUNK = 512
F32 = jnp.float32
BF16 = jnp.bfloat16
VMEM = pltpu.MemorySpace.VMEM


def shift(size, step):
    return [(i, (i + step) % size) for i in range(size)]


CORES = [(i, i ^ 1) for i in range(DP)]
ROWS = [[8 * y + o for o in range(8)] for y in range(4)]
PLANES = [[(8 * y + o) * MP + z for y in range(4) for z in range(MP)] for o in range(8)]


def along(base, size, step):
    span = base * size
    return [(i, i // span * span + (i + base * step) % span) for i in range(DP)]


def after(x, *others):
    return lax.optimization_barrier((x,) + others)[0]


def terms(x):
    first = x.astype(BF16).astype(F32)
    rest = x - first
    second = rest.astype(BF16).astype(F32)
    return first, second, rest - second


def split3(x):
    return jnp.concatenate(terms(x), axis=0).astype(BF16)


def fold3(x):
    rows = x.shape[0] // 3
    return (x[2 * rows :] + x[rows : 2 * rows]) + x[:rows]


def dot(a, b, left, right):
    return lax.dot_general(a, b, (((left,), (right,)), ((), ())), preferred_element_type=F32)


def local(kernel, out, *args, spaces=None, mib=8, scratch=(), **kw):
    spaces = spaces or [VMEM] * len(args)
    return pl.pallas_call(
        kernel,
        out_shape=out,
        in_specs=[pl.BlockSpec(memory_space=s) for s in spaces],
        out_specs=jax.tree.map(lambda _: pl.BlockSpec(memory_space=VMEM), out),
        scratch_shapes=scratch,
        compiler_params=pltpu.CompilerParams(vmem_limit_bytes=mib << 20),
        **kw,
    )(*args)


def shape(*dims, dtype=F32):
    return jax.ShapeDtypeStruct(dims, dtype)


def pieces(size, count):
    step = size // count
    return [slice(i * step, (i + 1) * step) for i in range(count)]


def kept(x):
    return pltpu.with_memory_space_constraint(x, VMEM)


def far(x):
    return pltpu.with_memory_space_constraint(x, pltpu.MemorySpace.HBM)


def reduce_kernel(q_ref, g_ref, out_ref, q_held, held, sems):
    first = pltpu.make_async_copy(q_ref, q_held, sems.at[0])
    first.start()
    copies = [pltpu.make_async_copy(g_ref.at[at], held.at[at], sems.at[1 + i]) for i, at in enumerate(pieces(TOKENS, 4))]
    for copy in copies:
        copy.start()
    first.wait()
    q = split3(q_held[...])
    for i, (copy, at) in enumerate(zip(copies, pieces(TOKENS, 4))):
        copy.wait()
        value = fold3(dot(q, held[at], 1, 1))
        out_ref[2 * i] = value[:, :128]
        out_ref[2 * i + 1] = value[:, 128:]


def error_left_kernel(q_ref, err_ref, out_ref, q_held, held, sems):
    depth = err_ref.shape[0]
    first = pltpu.make_async_copy(q_ref, q_held, sems.at[0])
    first.start()
    copies = [pltpu.make_async_copy(err_ref.at[at], held.at[at], sems.at[1 + i]) for i, at in enumerate(pieces(depth, 4))]
    for copy in copies:
        copy.start()
    first.wait()
    q = split3(q_held[...])
    for copy, at in zip(copies, pieces(depth, 4)):
        copy.wait()
        out_ref[:, at] = fold3(dot(q, held[at], 1, 1))


def left_kernel(parts_ref, x_ref, more_ref, out_ref):
    reduced = jnp.sum(parts_ref[...], axis=0)
    value = fold3(dot(split3(reduced), x_ref[...], 1, 0)) + more_ref[...]
    for z in range(MP):
        out_ref[z] = value[:, z * 256 : (z + 1) * 256]


def sum_spread_kernel(parts_ref, out_ref):
    value = jnp.sum(parts_ref[...], axis=0)
    out_ref[...] = jnp.broadcast_to(value[None], out_ref.shape)


def gram_schmidt_kernel(parts_ref, out_ref):
    rows = jnp.concatenate([parts_ref[z] for z in range(MP)], axis=1)
    index = lax.broadcasted_iota(jnp.int32, (R, 1), 0)
    for i in range(R):
        vector = rows[i : i + 1]
        products = jnp.sum(rows * vector, axis=1, keepdims=True)
        scale = 1.0 / jnp.sqrt(products[i : i + 1] + 1e-06)
        vector = vector * scale
        rows = jnp.where(index > i, rows - (products * scale) * vector, jnp.where(index == i, vector, rows))
    out_ref[...] = rows


def right_kernel(p_ref, err_ref, g_ref, *refs):
    blocks, (keep_ref, send_ref, rows_ref, grads_ref, held_ref, sems) = refs[:9], refs[9:]
    me = lax.axis_index("mp")
    starts = [me * 128]
    for step in range(1, 4):
        starts += [lax.rem(me + MP - step, MP) * 128, lax.rem(me + step, MP) * 128]
    last = lax.rem(me + 4, MP) * 128
    starts += [last, last + 64]
    copies = []
    for i, (block, start) in enumerate(zip(blocks, starts)):
        size = block.shape[0]
        copies.append(pltpu.make_async_copy(block, rows_ref.at[pl.ds(pl.multiple_of(start, size), size)], sems.at[i]))
    copies.append(pltpu.make_async_copy(g_ref, grads_ref, sems.at[9]))
    copies.append(pltpu.make_async_copy(err_ref, held_ref, sems.at[10]))
    for copy in copies:
        copy.start()
    left = split3(p_ref[...])
    for copy in copies[:9]:
        copy.wait()
    projected = fold3(dot(left, rows_ref[...], 1, 1))
    copies[9].wait()
    value = fold3(dot(split3(projected), grads_ref[...], 1, 0))
    copies[10].wait()
    value = value + fold3(dot(left, held_ref[...], 1, 0))
    first = value[:, :HALF]
    second = jnp.concatenate([value[:, HALF:], jnp.zeros((R, 2 * HALF - value.shape[1]), F32)], axis=1)
    core = lax.rem(lax.axis_index("dp"), 2)
    keep_ref[...] = jnp.where(core == 0, first, second)
    send_ref[...] = jnp.where(core == 0, second, first)


def merged_kernel(part, rows_ref, grads_ref, err_ref, out_ref):
    at = pl.ds(part * CHUNK, CHUNK)
    out_ref[...] = dot(rows_ref[:, at], grads_ref[...], 0, 0) + err_ref[at].astype(F32)


def add_kernel(a_ref, b_ref, out_ref):
    out_ref[...] = a_ref[...] + b_ref[...]


def add4_kernel(scale, own_ref, across_ref, one_ref, other_ref, out_ref):
    out_ref[...] = ((own_ref[...] + across_ref[...]) + (one_ref[...] + other_ref[...])) * scale


def residue_kernel(p_ref, mine_ref, other_ref, *refs):
    merged, (out_ref, q_ref, held, sems) = refs[:-4], refs[-4:]
    core = lax.rem(lax.axis_index("dp"), 2)
    mine, other = mine_ref[...], other_ref[...]
    first = jnp.where(core == 0, mine, other)
    second = jnp.where(core == 0, other, mine)
    q = jnp.concatenate([first, second[:, : q_ref.shape[1] - HALF]], axis=1)
    q_ref[...] = q
    a, b, c = terms(q)
    right = jnp.concatenate([a, b, c, a, b, a], axis=0).astype(BF16)
    copies = []
    for i, part in enumerate(merged):
        at = pl.ds(i * CHUNK, CHUNK)
        a, b, c = terms(p_ref[:, at])
        left = jnp.concatenate([a, a, a, b, b, c], axis=0).astype(BF16)
        held[i] = (part[...] - dot(left, right, 0, 0)).astype(BF16)
        copies.append(pltpu.make_async_copy(held.at[i], out_ref.at[at], sems.at[i]))
        copies[-1].start()
    for copy in copies:
        copy.wait()


def exchange(x, axis, groups=None):
    return lax.all_to_all(x, axis, 0, 0, axis_index_groups=groups)


def on_device(tokens, out_grad, error, q_prev):
    err = error[0]
    depth, columns = err.shape
    half = tokens.shape[0] // 2

    def pass_on(right, left):
        return lax.ppermute(right, "mp", shift(MP, 1)), lax.ppermute(left, "mp", shift(MP, -1))

    right1, left1 = pass_on(tokens, tokens)
    hbm = pltpu.MemorySpace.HBM
    dma = pltpu.SemaphoreType.DMA
    held = pltpu.VMEM((R, columns), F32)
    reduced = local(
        reduce_kernel, shape(MP, R, 128), far(q_prev), far(out_grad), spaces=[hbm, hbm], scratch=[held, pltpu.VMEM(out_grad.shape, BF16), dma((5,))]
    )
    more = local(
        error_left_kernel, shape(R, depth), far(q_prev), far(err), spaces=[hbm, hbm], scratch=[held, pltpu.VMEM(err.shape, BF16), dma((5,))]
    )
    reduced = exchange(reduced, "mp")
    part = local(left_kernel, shape(MP, R, 256), reduced, tokens, more)
    right2, left2 = pass_on(after(right1, part), after(left1, part))
    part = exchange(after(part, right1, left1), "dp", ROWS)
    part = local(sum_spread_kernel, shape(DP, R, 256), part)
    right3, left3 = pass_on(after(right2, part), after(left2, part))
    part = exchange(after(part, right2, left2), ("dp", "mp"), PLANES)
    part = local(sum_spread_kernel, shape(MP, R, 256), part)
    right4, left4 = pass_on(after(right3, part)[:half], after(left3, part)[half:])
    part = exchange(after(part, right3, left3), "dp", ROWS)
    p_factor = local(gram_schmidt_kernel, pltpu.VMEM((R, depth), F32), part)
    blocks = (tokens, right1, left1, right2, left2, right3, left3, right4, left4)

    keep, send, rows, grads, near = local(
        right_kernel,
        (
            shape(R, HALF),
            shape(R, HALF),
            pltpu.VMEM((TOKENS, depth), BF16),
            pltpu.VMEM((TOKENS, columns), BF16),
            pltpu.VMEM((depth, columns), BF16),
        ),
        kept(p_factor),
        far(err),
        far(out_grad),
        *blocks,
        spaces=[VMEM, hbm, hbm] + [pl.ANY] * 9,
        scratch=[dma((11,))],
    )
    rows, grads, near = kept(rows), kept(grads), kept(near)
    merged = [
        local(functools.partial(merged_kernel, i), pltpu.VMEM((CHUNK, columns), F32), rows, grads, near) for i in range(depth // CHUNK)
    ]
    mine = local(add_kernel, shape(R, HALF), after(keep, merged[0]), lax.ppermute(send, "dp", CORES))
    for base, scale, beside in ((2, 1.0, merged[1:]), (8, 1.0 / DP, [])):
        one, other, across = (lax.ppermute(mine, "dp", along(base, 4, step)) for step in (1, 3, 2))
        mine = after(mine, *beside)
        mine = local(functools.partial(add4_kernel, scale), shape(R, HALF), mine, across, one, other)
    other = lax.ppermute(mine, "dp", CORES)
    new_error, q_factor = pl.pallas_call(
        residue_kernel,
        out_shape=(shape(depth, columns, dtype=BF16), shape(R, columns)),
        in_specs=[pl.BlockSpec(memory_space=VMEM)] * (3 + len(merged)),
        out_specs=(pl.BlockSpec(memory_space=hbm), pl.BlockSpec(memory_space=VMEM)),
        scratch_shapes=[pltpu.VMEM((len(merged), CHUNK, columns), BF16), dma((len(merged),))],
        compiler_params=pltpu.CompilerParams(vmem_limit_bytes=12 << 20),
    )(kept(p_factor), mine, other, *[kept(part) for part in merged])
    return (p_factor, q_factor, new_error[None])


def solution(mesh):
    placed = (P(("dp", "mp"), None), P("dp", "mp"), P("dp", None, "mp"), P(None, "mp"))
    return jax.shard_map(
        on_device,
        mesh=mesh,
        in_specs=placed,
        out_specs=(P(), P(None, "mp"), P("dp", None, "mp")),
        check_vma=False,
    )
```

```python
import functools

import jax
import jax.numpy as jnp
from jax import lax
from jax.experimental import pallas as pl
from jax.experimental.pallas import tpu as pltpu
from jax.sharding import PartitionSpec as P

MP = 8
DP = 32
R = 8
HALF = 512
TOKENS = 1024
CHUNK = 512
F32 = jnp.float32
BF16 = jnp.bfloat16
VMEM = pltpu.MemorySpace.VMEM


def shift(size, step):
    return [(i, (i + step) % size) for i in range(size)]


CORES = [(i, i ^ 1) for i in range(DP)]
CHIPS = [[2 * i for i in range(DP // 2)], [2 * i + 1 for i in range(DP // 2)]]


def along(base, size, step):
    span = base * size
    return [(i, i // span * span + (i + base * step) % span) for i in range(DP)]


def after(x, *others):
    return lax.optimization_barrier((x,) + others)[0]


def terms(x):
    first = x.astype(BF16).astype(F32)
    rest = x - first
    second = rest.astype(BF16).astype(F32)
    return first, second, rest - second


def split3(x):
    return jnp.concatenate(terms(x), axis=0).astype(BF16)


def fold3(x):
    rows = x.shape[0] // 3
    return (x[2 * rows :] + x[rows : 2 * rows]) + x[:rows]


def dot(a, b, left, right):
    return lax.dot_general(a, b, (((left,), (right,)), ((), ())), preferred_element_type=F32)


def local(kernel, out, *args, spaces=None, mib=8, scratch=(), **kw):
    spaces = spaces or [VMEM] * len(args)
    return pl.pallas_call(
        kernel,
        out_shape=out,
        in_specs=[pl.BlockSpec(memory_space=s) for s in spaces],
        out_specs=jax.tree.map(lambda _: pl.BlockSpec(memory_space=VMEM), out),
        scratch_shapes=scratch,
        compiler_params=pltpu.CompilerParams(vmem_limit_bytes=mib << 20),
        **kw,
    )(*args)


def shape(*dims, dtype=F32):
    return jax.ShapeDtypeStruct(dims, dtype)


def pieces(size, count):
    step = size // count
    return [slice(i * step, (i + 1) * step) for i in range(count)]


def kept(x):
    return pltpu.with_memory_space_constraint(x, VMEM)


def far(x):
    return pltpu.with_memory_space_constraint(x, pltpu.MemorySpace.HBM)


def reduce_kernel(q_ref, g_ref, out_ref, q_held, held, sems):
    first = pltpu.make_async_copy(q_ref, q_held, sems.at[0])
    first.start()
    parts = pieces(TOKENS, 2)
    copies = [pltpu.make_async_copy(g_ref.at[at], held.at[at], sems.at[1 + i]) for i, at in enumerate(parts)]
    for copy in copies:
        copy.start()
    first.wait()
    q = split3(q_held[...])
    for i, (copy, at) in enumerate(zip(copies, parts)):
        copy.wait()
        value = fold3(dot(q, held[at], 1, 1))
        for j in range(4):
            out_ref[4 * i + j] = value[:, j * 128 : (j + 1) * 128]


def error_left_kernel(q_ref, err_ref, out_ref, q_held, held, sems):
    depth = err_ref.shape[0]
    first = pltpu.make_async_copy(q_ref, q_held, sems.at[0])
    first.start()
    copies = [pltpu.make_async_copy(err_ref.at[at], held.at[at], sems.at[1 + i]) for i, at in enumerate(pieces(depth, 4))]
    for copy in copies:
        copy.start()
    first.wait()
    q = split3(q_held[...])
    for copy, at in zip(copies, pieces(depth, 4)):
        copy.wait()
        out_ref[:, at] = fold3(dot(q, held[at], 1, 1))


def left_kernel(parts_ref, x_ref, more_ref, out_ref):
    reduced = jnp.sum(parts_ref[...], axis=0)
    value = fold3(dot(split3(reduced), x_ref[...], 1, 0)) + more_ref[...]
    for i in range(out_ref.shape[0]):
        out_ref[i] = value[:, i * 128 : (i + 1) * 128]


def sum_kernel(parts_ref, out_ref):
    out_ref[...] = jnp.sum(parts_ref[...], axis=0)


def add_spread_kernel(a_ref, b_ref, out_ref):
    out_ref[...] = jnp.broadcast_to((a_ref[...] + b_ref[...])[None], out_ref.shape)


def sum_spread_kernel(parts_ref, out_ref):
    value = jnp.sum(parts_ref[...], axis=0)
    out_ref[...] = jnp.broadcast_to(value[None], out_ref.shape)


def gram_schmidt(rows):
    index = lax.broadcasted_iota(jnp.int32, (R, 1), 0)
    for i in range(R):
        vector = rows[i : i + 1]
        products = jnp.sum(rows * vector, axis=1, keepdims=True)
        scale = 1.0 / jnp.sqrt(products[i : i + 1] + 1e-06)
        vector = vector * scale
        rows = jnp.where(index > i, rows - (products * scale) * vector, jnp.where(index == i, vector, rows))
    return rows


def right_kernel(parts_ref, err_ref, g_ref, *refs):
    blocks, (p_ref, keep_ref, send_ref, rows_ref, grads_ref, held_ref, sems) = refs[:9], refs[9:]
    me = lax.axis_index("mp")
    starts = [me * 128]
    for step in range(1, 4):
        starts += [lax.rem(me + MP - step, MP) * 128, lax.rem(me + step, MP) * 128]
    last = lax.rem(me + 4, MP) * 128
    starts += [last, last + 64]
    copies = []
    for i, (block, start) in enumerate(zip(blocks, starts)):
        size = block.shape[0]
        copies.append(pltpu.make_async_copy(block, rows_ref.at[pl.ds(pl.multiple_of(start, size), size)], sems.at[i]))
    copies.append(pltpu.make_async_copy(g_ref, grads_ref, sems.at[9]))
    copies.append(pltpu.make_async_copy(err_ref, held_ref, sems.at[10]))
    for copy in copies:
        copy.start()
    p = gram_schmidt(jnp.concatenate([parts_ref[i] for i in range(parts_ref.shape[0])], axis=1))
    p_ref[...] = p
    left = split3(p)
    for copy in copies[:9]:
        copy.wait()
    projected = fold3(dot(left, rows_ref[...], 1, 1))
    copies[9].wait()
    value = fold3(dot(split3(projected), grads_ref[...], 1, 0))
    copies[10].wait()
    value = value + fold3(dot(left, held_ref[...], 1, 0))
    first = value[:, :HALF]
    second = jnp.concatenate([value[:, HALF:], jnp.zeros((R, 2 * HALF - value.shape[1]), F32)], axis=1)
    core = lax.rem(lax.axis_index("dp"), 2)
    keep_ref[...] = jnp.where(core == 0, first, second)
    send_ref[...] = jnp.where(core == 0, second, first)


def merged_kernel(part, rows_ref, grads_ref, err_ref, out_ref):
    at = pl.ds(part * CHUNK, CHUNK)
    out_ref[...] = dot(rows_ref[:, at], grads_ref[...], 0, 0) + err_ref[at].astype(F32)


def add_kernel(a_ref, b_ref, out_ref):
    out_ref[...] = a_ref[...] + b_ref[...]


def add4_kernel(scale, own_ref, across_ref, one_ref, other_ref, out_ref):
    out_ref[...] = ((own_ref[...] + across_ref[...]) + (one_ref[...] + other_ref[...])) * scale


def residue_kernel(p_ref, mine_ref, other_ref, *refs):
    merged, (out_ref, q_ref, held, sems) = refs[:-4], refs[-4:]
    core = lax.rem(lax.axis_index("dp"), 2)
    mine, other = mine_ref[...], other_ref[...]
    first = jnp.where(core == 0, mine, other)
    second = jnp.where(core == 0, other, mine)
    q = jnp.concatenate([first, second[:, : q_ref.shape[1] - HALF]], axis=1)
    q_ref[...] = q
    a, b, c = terms(q)
    right = jnp.concatenate([a, b, c, a, b, a], axis=0).astype(BF16)
    copies = []
    for i, part in enumerate(merged):
        at = pl.ds(i * CHUNK, CHUNK)
        a, b, c = terms(p_ref[:, at])
        left = jnp.concatenate([a, a, a, b, b, c], axis=0).astype(BF16)
        held[i] = (part[...] - dot(left, right, 0, 0)).astype(BF16)
        copies.append(pltpu.make_async_copy(held.at[i], out_ref.at[at], sems.at[i]))
        copies[-1].start()
    for copy in copies:
        copy.wait()


def exchange(x, axis, groups=None):
    return lax.all_to_all(x, axis, 0, 0, axis_index_groups=groups)


def on_device(tokens, out_grad, error, q_prev):
    err = error[0]
    depth, columns = err.shape
    half = tokens.shape[0] // 2

    def pass_on(right, left):
        return lax.ppermute(right, "mp", shift(MP, 1)), lax.ppermute(left, "mp", shift(MP, -1))

    right1, left1 = pass_on(tokens, tokens)
    hbm = pltpu.MemorySpace.HBM
    dma = pltpu.SemaphoreType.DMA
    held = pltpu.VMEM((R, columns), F32)
    reduced = local(
        reduce_kernel, shape(MP, R, 128), far(q_prev), far(out_grad), spaces=[hbm, hbm], scratch=[held, pltpu.VMEM(out_grad.shape, BF16), dma((5,))]
    )
    more = local(
        error_left_kernel, shape(R, depth), far(q_prev), far(err), spaces=[hbm, hbm], scratch=[held, pltpu.VMEM(err.shape, BF16), dma((5,))]
    )
    reduced = exchange(reduced, "mp")
    part = local(left_kernel, shape(DP // 2, R, 128), reduced, tokens, more)
    right2, left2 = pass_on(after(right1, part), after(left1, part))
    part = local(sum_kernel, shape(R, 128), exchange(after(part, right1, left1), "dp", CHIPS))
    right3, left3 = pass_on(after(right2, part), after(left2, part))
    part = local(add_spread_kernel, shape(MP, R, 128), part, lax.ppermute(part, "dp", CORES))
    part = exchange(after(part, right2, left2), "mp")
    part = local(sum_spread_kernel, shape(DP // 2, R, 128), part)
    right4, left4 = pass_on(after(right3, part)[:half], after(left3, part)[half:])
    part = exchange(after(part, right3, left3), "dp", CHIPS)
    blocks = (tokens, right1, left1, right2, left2, right3, left3, right4, left4)

    p_factor, keep, send, rows, grads, near = local(
        right_kernel,
        (
            pltpu.VMEM((R, depth), F32),
            shape(R, HALF),
            shape(R, HALF),
            pltpu.VMEM((TOKENS, depth), BF16),
            pltpu.VMEM((TOKENS, columns), BF16),
            pltpu.VMEM((depth, columns), BF16),
        ),
        part,
        far(err),
        far(out_grad),
        *blocks,
        spaces=[VMEM, hbm, hbm] + [pl.ANY] * 9,
        scratch=[dma((11,))],
    )
    rows, grads, near = kept(rows), kept(grads), kept(near)
    merged = [
        local(functools.partial(merged_kernel, i), pltpu.VMEM((CHUNK, columns), F32), rows, grads, near) for i in range(depth // CHUNK)
    ]
    mine = local(add_kernel, shape(R, HALF), after(keep, merged[0]), lax.ppermute(send, "dp", CORES))
    for base, scale, beside in ((2, 1.0, merged[1:3]), (8, 1.0 / DP, merged[3:])):
        one, other, across = (lax.ppermute(mine, "dp", along(base, 4, step)) for step in (1, 3, 2))
        mine = after(mine, *beside)
        mine = local(functools.partial(add4_kernel, scale), shape(R, HALF), mine, across, one, other)
    other = lax.ppermute(mine, "dp", CORES)
    new_error, q_factor = pl.pallas_call(
        residue_kernel,
        out_shape=(shape(depth, columns, dtype=BF16), shape(R, columns)),
        in_specs=[pl.BlockSpec(memory_space=VMEM)] * (3 + len(merged)),
        out_specs=(pl.BlockSpec(memory_space=hbm), pl.BlockSpec(memory_space=VMEM)),
        scratch_shapes=[pltpu.VMEM((len(merged), CHUNK, columns), BF16), dma((len(merged),))],
        compiler_params=pltpu.CompilerParams(vmem_limit_bytes=12 << 20),
    )(kept(p_factor), mine, other, *[kept(part) for part in merged])
    return (p_factor, q_factor, new_error[None])


def solution(mesh):
    placed = (P(("dp", "mp"), None), P("dp", "mp"), P("dp", None, "mp"), P(None, "mp"))
    return jax.shard_map(
        on_device,
        mesh=mesh,
        in_specs=placed,
        out_specs=(P(), P(None, "mp"), P("dp", None, "mp")),
        check_vma=False,
    )
```

```python
import functools

import jax
import jax.numpy as jnp
from jax import lax
from jax.experimental import pallas as pl
from jax.experimental.pallas import tpu as pltpu
from jax.sharding import PartitionSpec as P

MP = 8
DP = 32
R = 8
TOKENS = 1024
CHUNK = 512
F32 = jnp.float32
BF16 = jnp.bfloat16
VMEM = pltpu.MemorySpace.VMEM


def shift(size, step):
    return [(i, (i + step) % size) for i in range(size)]


CORES = [(i, i ^ 1) for i in range(DP)]
CHIPS = [[2 * i for i in range(DP // 2)], [2 * i + 1 for i in range(DP // 2)]]


def along(base, size, step):
    span = base * size
    return [(i, i // span * span + (i + base * step) % span) for i in range(DP)]


def after(x, *others):
    return lax.optimization_barrier((x,) + others)[0]


def terms(x):
    first = x.astype(BF16).astype(F32)
    rest = x - first
    second = rest.astype(BF16).astype(F32)
    return first, second, rest - second


def split3(x):
    return jnp.concatenate(terms(x), axis=0).astype(BF16)


def fold3(x):
    rows = x.shape[0] // 3
    return (x[2 * rows :] + x[rows : 2 * rows]) + x[:rows]


def dot(a, b, left, right):
    return lax.dot_general(a, b, (((left,), (right,)), ((), ())), preferred_element_type=F32)


def local(kernel, out, *args, spaces=None, mib=8, scratch=(), **kw):
    spaces = spaces or [VMEM] * len(args)
    return pl.pallas_call(
        kernel,
        out_shape=out,
        in_specs=[pl.BlockSpec(memory_space=s) for s in spaces],
        out_specs=jax.tree.map(lambda _: pl.BlockSpec(memory_space=VMEM), out),
        scratch_shapes=scratch,
        compiler_params=pltpu.CompilerParams(vmem_limit_bytes=mib << 20),
        **kw,
    )(*args)


def shape(*dims, dtype=F32):
    return jax.ShapeDtypeStruct(dims, dtype)


def pieces(size, count):
    step = size // count
    return [slice(i * step, (i + 1) * step) for i in range(count)]


def kept(x):
    return pltpu.with_memory_space_constraint(x, VMEM)


def far(x):
    return pltpu.with_memory_space_constraint(x, pltpu.MemorySpace.HBM)


def reduce_kernel(q_ref, g_ref, out_ref, q_held, held, sems):
    first = pltpu.make_async_copy(q_ref, q_held, sems.at[0])
    first.start()
    parts = pieces(TOKENS, 2)
    copies = [pltpu.make_async_copy(g_ref.at[at], held.at[at], sems.at[1 + i]) for i, at in enumerate(parts)]
    for copy in copies:
        copy.start()
    first.wait()
    q = split3(q_held[...])
    for i, (copy, at) in enumerate(zip(copies, parts)):
        copy.wait()
        value = fold3(dot(q, held[at], 1, 1))
        for j in range(4):
            out_ref[4 * i + j] = value[:, j * 128 : (j + 1) * 128]


def error_left_kernel(q_ref, err_ref, out_ref, q_held, held, sems):
    depth = err_ref.shape[0]
    first = pltpu.make_async_copy(q_ref, q_held, sems.at[0])
    first.start()
    copies = [pltpu.make_async_copy(err_ref.at[at], held.at[at], sems.at[1 + i]) for i, at in enumerate(pieces(depth, 4))]
    for copy in copies:
        copy.start()
    first.wait()
    q = split3(q_held[...])
    for copy, at in zip(copies, pieces(depth, 4)):
        copy.wait()
        out_ref[:, at] = fold3(dot(q, held[at], 1, 1))


def left_kernel(parts_ref, x_ref, more_ref, out_ref):
    reduced = jnp.sum(parts_ref[...], axis=0)
    value = fold3(dot(split3(reduced), x_ref[...], 1, 0)) + more_ref[...]
    for i in range(out_ref.shape[0]):
        out_ref[i] = value[:, i * 128 : (i + 1) * 128]


def sum_kernel(parts_ref, out_ref):
    out_ref[...] = jnp.sum(parts_ref[...], axis=0)


def add_spread_kernel(a_ref, b_ref, out_ref):
    out_ref[...] = jnp.broadcast_to((a_ref[...] + b_ref[...])[None], out_ref.shape)


def sum_spread_kernel(parts_ref, out_ref):
    value = jnp.sum(parts_ref[...], axis=0)
    out_ref[...] = jnp.broadcast_to(value[None], out_ref.shape)


def gram_schmidt(rows):
    index = lax.broadcasted_iota(jnp.int32, (R, 1), 0)
    for i in range(R):
        vector = rows[i : i + 1]
        products = jnp.sum(rows * vector, axis=1, keepdims=True)
        scale = 1.0 / jnp.sqrt(products[i : i + 1] + 1e-06)
        vector = vector * scale
        rows = jnp.where(index > i, rows - (products * scale) * vector, jnp.where(index == i, vector, rows))
    return rows


def starts_of():
    me = lax.axis_index("mp")
    owners = [me]
    for step in range(1, 4):
        owners += [lax.rem(me + MP - step, MP), lax.rem(me + step, MP)]
    owners.append(lax.rem(me + 4, MP))
    return [pl.multiple_of(owner * 128, 128) for owner in owners]


def right_kernel(parts_ref, err_ref, g_ref, *refs):
    blocks, (p_ref, value_ref, projected_ref, rows_ref, grads_ref, held_ref, sems) = refs[:7], refs[7:]
    copies = []
    for i, (block, start) in enumerate(zip(blocks, starts_of())):
        copies.append(pltpu.make_async_copy(block, rows_ref.at[pl.ds(start, 128)], sems.at[i]))
    copies.append(pltpu.make_async_copy(err_ref, held_ref, sems.at[7]))
    copies.append(pltpu.make_async_copy(g_ref, grads_ref, sems.at[8]))
    for copy in copies:
        copy.start()
    rows_ref[pl.ds(starts_of()[7], 128)] = jnp.zeros((128, rows_ref.shape[1]), BF16)
    p = gram_schmidt(jnp.concatenate([parts_ref[i] for i in range(parts_ref.shape[0])], axis=1))
    p_ref[...] = p
    left = split3(p)
    for copy in copies[:7]:
        copy.wait()
    projected_ref[...] = fold3(dot(left, rows_ref[...], 1, 1))
    copies[7].wait()
    value_ref[...] = fold3(dot(left, held_ref[...], 1, 0))
    copies[8].wait()


def right_last_kernel(p_ref, value_ref, projected_ref, grads_ref, block_ref, old_ref, out_ref, rows_ref, total, sem):
    del old_ref
    start = starts_of()[7]
    copy = pltpu.make_async_copy(block_ref, rows_ref.at[pl.ds(start, 128)], sem)
    copy.start()
    total[...] = projected_ref[...]
    total[:, pl.ds(start, 128)] = fold3(dot(split3(p_ref[...]), block_ref[...], 1, 1))
    out_ref[...] = value_ref[...] + fold3(dot(split3(total[...]), grads_ref[...], 1, 0))
    copy.wait()


def merged_kernel(part, p_ref, rows_ref, grads_ref, err_ref, out_ref, left_ref):
    at = pl.ds(part * CHUNK, CHUNK)
    a, b, c = terms(p_ref[:, at])
    left_ref[...] = jnp.concatenate([a, a, a, b, b, c], axis=0).T.astype(BF16)
    out_ref[...] = dot(rows_ref[:, at], grads_ref[...], 0, 0) + err_ref[at].astype(F32)


def add4_kernel(own_ref, across_ref, one_ref, other_ref, out_ref):
    out_ref[...] = (own_ref[...] + across_ref[...]) + (one_ref[...] + other_ref[...])


def residue_kernel(mine_ref, other_ref, *refs):
    merged, lefts, (out_ref, q_ref, held, sems) = refs[:4], refs[4:8], refs[8:]
    q = (mine_ref[...] + other_ref[...]) / DP
    q_ref[...] = q
    a, b, c = terms(q)
    right = jnp.concatenate([a, b, c, a, b, a], axis=0).astype(BF16)
    copies = []
    for i, (part, left) in enumerate(zip(merged, lefts)):
        at = pl.ds(i * CHUNK, CHUNK)
        held[i] = (part[...] - dot(left[...], right, 1, 0)).astype(BF16)
        copies.append(pltpu.make_async_copy(held.at[i], out_ref.at[at], sems.at[i]))
        copies[-1].start()
    for copy in copies:
        copy.wait()


def exchange(x, axis, groups=None):
    return lax.all_to_all(x, axis, 0, 0, axis_index_groups=groups)


def on_device(tokens, out_grad, error, q_prev):
    err = error[0]
    depth, columns = err.shape

    def rightward(x):
        return lax.ppermute(x, "mp", shift(MP, 1))

    def leftward(x):
        return lax.ppermute(x, "mp", shift(MP, -1))

    right1 = rightward(tokens)
    hbm = pltpu.MemorySpace.HBM
    dma = pltpu.SemaphoreType.DMA
    held = pltpu.VMEM((R, columns), F32)
    reduced = local(
        reduce_kernel, shape(MP, R, 128), far(q_prev), far(out_grad), spaces=[hbm, hbm], scratch=[held, pltpu.VMEM(out_grad.shape, BF16), dma((5,))]
    )
    left1 = leftward(after(tokens, reduced))
    more = local(
        error_left_kernel, shape(R, depth), far(q_prev), far(err), spaces=[hbm, hbm], scratch=[held, pltpu.VMEM(err.shape, BF16), dma((5,))]
    )
    reduced = exchange(reduced, "mp")
    part = local(left_kernel, shape(DP // 2, R, 128), reduced, tokens, more)
    right2 = rightward(after(right1, part))
    part = local(sum_kernel, shape(R, 128), exchange(after(part, right1), "dp", CHIPS))
    right3, left2 = rightward(after(right2, part)), leftward(after(left1, part))
    part = local(add_spread_kernel, shape(MP, R, 128), part, lax.ppermute(part, "dp", CORES))
    part = exchange(after(part, right2, left1), "mp")
    part = local(sum_spread_kernel, shape(DP // 2, R, 128), part)
    right4, left3 = rightward(after(right3, part)), leftward(after(left2, part))
    part = exchange(after(part, right3, left2), "dp", CHIPS)
    blocks = (tokens, right1, left1, right2, left2, right3, left3)
    p_factor, value, projected, rows, grads, near = local(
        right_kernel,
        (
            pltpu.VMEM((R, depth), F32),
            pltpu.VMEM((R, columns), F32),
            pltpu.VMEM((R, TOKENS), F32),
            pltpu.VMEM((TOKENS, depth), BF16),
            pltpu.VMEM((TOKENS, columns), BF16),
            pltpu.VMEM((depth, columns), BF16),
        ),
        part,
        far(err),
        far(out_grad),
        *blocks,
        spaces=[VMEM, hbm, hbm] + [pl.ANY] * 7,
        scratch=[dma((9,))],
    )
    p, grads, near = kept(p_factor), kept(grads), kept(near)
    mine, rows = local(
        right_last_kernel,
        (shape(R, columns), pltpu.VMEM((TOKENS, depth), BF16)),
        p,
        kept(value),
        kept(projected),
        grads,
        right4,
        kept(rows),
        scratch=[pltpu.VMEM((R, TOKENS), F32), dma],
        input_output_aliases={5: 1},
    )
    rows = kept(rows)
    out = (pltpu.VMEM((CHUNK, columns), F32), pltpu.VMEM((CHUNK, 6 * R), BF16))
    merged, lefts = zip(*[local(functools.partial(merged_kernel, i), out, p, rows, grads, near) for i in range(depth // CHUNK)])
    for base, beside in ((2, merged[:2]), (8, merged[2:])):
        one, other, across = (lax.ppermute(mine, "dp", along(base, 4, step)) for step in (1, 3, 2))
        mine = local(add4_kernel, shape(R, columns), after(mine, *beside), across, one, other)
    other = lax.ppermute(mine, "dp", CORES)
    new_error, q_factor = pl.pallas_call(
        residue_kernel,
        out_shape=(shape(depth, columns, dtype=BF16), shape(R, columns)),
        in_specs=[pl.BlockSpec(memory_space=VMEM)] * (2 + 2 * len(merged)),
        out_specs=(pl.BlockSpec(memory_space=hbm), pl.BlockSpec(memory_space=VMEM)),
        scratch_shapes=[pltpu.VMEM((len(merged), CHUNK, columns), BF16), dma((len(merged),))],
        compiler_params=pltpu.CompilerParams(vmem_limit_bytes=12 << 20),
    )(mine, other, *[kept(part) for part in merged + lefts])
    return (p_factor, q_factor, new_error[None])


def solution(mesh):
    placed = (P(("dp", "mp"), None), P("dp", "mp"), P("dp", None, "mp"), P(None, "mp"))
    return jax.shard_map(
        on_device,
        mesh=mesh,
        in_specs=placed,
        out_specs=(P(), P(None, "mp"), P("dp", None, "mp")),
        check_vma=False,
    )
```

```python
import functools

import jax
import jax.numpy as jnp
from jax import lax
from jax.experimental import pallas as pl
from jax.experimental.pallas import tpu as pltpu
from jax.sharding import PartitionSpec as P

MP = 8
DP = 32
R = 8
TOKENS = 1024
CHUNK = 1024
PIECE = 512
F32 = jnp.float32
BF16 = jnp.bfloat16
VMEM = pltpu.MemorySpace.VMEM


def shift(size, step):
    return [(i, (i + step) % size) for i in range(size)]


CORES = [(i, i ^ 1) for i in range(DP)]
CHIPS = [[2 * i for i in range(DP // 2)], [2 * i + 1 for i in range(DP // 2)]]


def along(base, size, step):
    span = base * size
    return [(i, i // span * span + (i + base * step) % span) for i in range(DP)]


def after(x, *others):
    return lax.optimization_barrier((x,) + others)[0]


def terms(x):
    first = x.astype(BF16).astype(F32)
    rest = x - first
    second = rest.astype(BF16).astype(F32)
    return first, second, rest - second


def split3(x):
    return jnp.concatenate(terms(x), axis=0).astype(BF16)


def fold3(x):
    rows = x.shape[0] // 3
    return (x[2 * rows :] + x[rows : 2 * rows]) + x[:rows]


def dot(a, b, left, right):
    return lax.dot_general(a, b, (((left,), (right,)), ((), ())), preferred_element_type=F32)


def local(kernel, out, *args, spaces=None, mib=8, scratch=(), **kw):
    spaces = spaces or [VMEM] * len(args)
    return pl.pallas_call(
        kernel,
        out_shape=out,
        in_specs=[pl.BlockSpec(memory_space=s) for s in spaces],
        out_specs=jax.tree.map(lambda _: pl.BlockSpec(memory_space=VMEM), out),
        scratch_shapes=scratch,
        compiler_params=pltpu.CompilerParams(vmem_limit_bytes=mib << 20),
        **kw,
    )(*args)


def shape(*dims, dtype=F32):
    return jax.ShapeDtypeStruct(dims, dtype)


def pieces(size, count):
    step = size // count
    return [slice(i * step, (i + 1) * step) for i in range(count)]


def kept(x):
    return pltpu.with_memory_space_constraint(x, VMEM)


def far(x):
    return pltpu.with_memory_space_constraint(x, pltpu.MemorySpace.HBM)


def reduce_kernel(q_ref, g_ref, out_ref, q_held, held, sems):
    first = pltpu.make_async_copy(q_ref, q_held, sems.at[0])
    first.start()
    parts = pieces(TOKENS, 2)
    copies = [pltpu.make_async_copy(g_ref.at[at], held.at[at], sems.at[1 + i]) for i, at in enumerate(parts)]
    for copy in copies:
        copy.start()
    first.wait()
    q = split3(q_held[...])
    for i, (copy, at) in enumerate(zip(copies, parts)):
        copy.wait()
        value = fold3(dot(q, held[at], 1, 1))
        for j in range(4):
            out_ref[4 * i + j] = value[:, j * 128 : (j + 1) * 128]


def error_left_kernel(q_ref, err_ref, out_ref, q_held, held, sems):
    depth = err_ref.shape[0]
    first = pltpu.make_async_copy(q_ref, q_held, sems.at[0])
    first.start()
    copies = [pltpu.make_async_copy(err_ref.at[at], held.at[at], sems.at[1 + i]) for i, at in enumerate(pieces(depth, 4))]
    for copy in copies:
        copy.start()
    first.wait()
    q = split3(q_held[...])
    for copy, at in zip(copies, pieces(depth, 4)):
        copy.wait()
        out_ref[:, at] = fold3(dot(q, held[at], 1, 1))


def left_kernel(parts_ref, x_ref, more_ref, out_ref):
    reduced = jnp.sum(parts_ref[...], axis=0)
    value = fold3(dot(split3(reduced), x_ref[...], 1, 0)) + more_ref[...]
    for i in range(out_ref.shape[0]):
        out_ref[i] = value[:, i * 128 : (i + 1) * 128]


def sum_kernel(parts_ref, out_ref):
    out_ref[...] = jnp.sum(parts_ref[...], axis=0)


def add_spread_kernel(a_ref, b_ref, out_ref):
    out_ref[...] = jnp.broadcast_to((a_ref[...] + b_ref[...])[None], out_ref.shape)


def sum_spread_kernel(parts_ref, out_ref):
    value = jnp.sum(parts_ref[...], axis=0)
    out_ref[...] = jnp.broadcast_to(value[None], out_ref.shape)


def gram_schmidt(rows):
    index = lax.broadcasted_iota(jnp.int32, (R, 1), 0)
    for i in range(R):
        vector = rows[i : i + 1]
        products = jnp.sum(rows * vector, axis=1, keepdims=True)
        scale = 1.0 / jnp.sqrt(products[i : i + 1] + 1e-06)
        vector = vector * scale
        rows = jnp.where(index > i, rows - (products * scale) * vector, jnp.where(index == i, vector, rows))
    return rows


def starts_of():
    me = lax.axis_index("mp")
    owners = [me]
    for step in range(1, 4):
        owners += [lax.rem(me + MP - step, MP), lax.rem(me + step, MP)]
    owners.append(lax.rem(me + 4, MP))
    return [pl.multiple_of(owner * 128, 128) for owner in owners]


def right_kernel(parts_ref, err_ref, g_ref, *refs):
    blocks, (p_ref, value_ref, projected_ref, rows_ref, grads_ref, held_ref, sems) = refs[:7], refs[7:]
    copies = []
    for i, (block, start) in enumerate(zip(blocks, starts_of())):
        copies.append(pltpu.make_async_copy(block, rows_ref.at[pl.ds(start, 128)], sems.at[i]))
    copies.append(pltpu.make_async_copy(err_ref, held_ref, sems.at[7]))
    copies.append(pltpu.make_async_copy(g_ref, grads_ref, sems.at[8]))
    for copy in copies:
        copy.start()
    rows_ref[pl.ds(starts_of()[7], 128)] = jnp.zeros((128, rows_ref.shape[1]), BF16)
    p = gram_schmidt(jnp.concatenate([parts_ref[i] for i in range(parts_ref.shape[0])], axis=1))
    p_ref[...] = p
    left = split3(p)
    for copy in copies[:7]:
        copy.wait()
    projected_ref[...] = fold3(dot(left, rows_ref[...], 1, 1))
    copies[7].wait()
    value_ref[...] = fold3(dot(left, held_ref[...], 1, 0))
    copies[8].wait()


def right_last_kernel(p_ref, value_ref, projected_ref, grads_ref, block_ref, old_ref, out_ref, rows_ref, total, sem):
    del old_ref
    start = starts_of()[7]
    copy = pltpu.make_async_copy(block_ref, rows_ref.at[pl.ds(start, 128)], sem)
    copy.start()
    total[...] = projected_ref[...]
    total[:, pl.ds(start, 128)] = fold3(dot(split3(p_ref[...]), block_ref[...], 1, 1))
    out_ref[...] = value_ref[...] + fold3(dot(split3(total[...]), grads_ref[...], 1, 0))
    copy.wait()


def merged_kernel(part, p_ref, rows_ref, grads_ref, err_ref, out_ref, left_ref):
    at = pl.ds(part * CHUNK, CHUNK)
    a, b, c = terms(p_ref[:, at])
    left_ref[...] = jnp.concatenate([a, a, a, b, b, c], axis=0).T.astype(BF16)
    out_ref[...] = dot(rows_ref[:, at], grads_ref[...], 0, 0) + err_ref[at].astype(F32)


def add4_kernel(own_ref, across_ref, one_ref, other_ref, out_ref):
    out_ref[...] = (own_ref[...] + across_ref[...]) + (one_ref[...] + other_ref[...])


def residue_kernel(mine_ref, other_ref, *refs):
    merged, lefts, (out_ref, q_ref, held, sems) = refs[:2], refs[2:4], refs[4:]
    q = (mine_ref[...] + other_ref[...]) / DP
    q_ref[...] = q
    a, b, c = terms(q)
    right = jnp.concatenate([a, b, c, a, b, a], axis=0).astype(BF16)
    copies = []
    for i in range(held.shape[0]):
        part, left = merged[i * PIECE // CHUNK], lefts[i * PIECE // CHUNK]
        inside = pl.ds(i * PIECE % CHUNK, PIECE)
        held[i] = (part[inside] - dot(left[inside], right, 1, 0)).astype(BF16)
        copies.append(pltpu.make_async_copy(held.at[i], out_ref.at[pl.ds(i * PIECE, PIECE)], sems.at[i]))
        copies[-1].start()
    for copy in copies:
        copy.wait()


def exchange(x, axis, groups=None):
    return lax.all_to_all(x, axis, 0, 0, axis_index_groups=groups)


def on_device(tokens, out_grad, error, q_prev):
    err = error[0]
    depth, columns = err.shape

    def rightward(x):
        return lax.ppermute(x, "mp", shift(MP, 1))

    def leftward(x):
        return lax.ppermute(x, "mp", shift(MP, -1))

    right1 = rightward(tokens)
    hbm = pltpu.MemorySpace.HBM
    dma = pltpu.SemaphoreType.DMA
    held = pltpu.VMEM((R, columns), F32)
    reduced = local(
        reduce_kernel, shape(MP, R, 128), far(q_prev), far(out_grad), spaces=[hbm, hbm], scratch=[held, pltpu.VMEM(out_grad.shape, BF16), dma((5,))]
    )
    left1 = leftward(after(tokens, reduced))
    more = local(
        error_left_kernel, shape(R, depth), far(q_prev), far(err), spaces=[hbm, hbm], scratch=[held, pltpu.VMEM(err.shape, BF16), dma((5,))]
    )
    reduced = exchange(reduced, "mp")
    part = local(left_kernel, shape(DP // 2, R, 128), reduced, tokens, more)
    right2 = rightward(after(right1, part))
    part = local(sum_kernel, shape(R, 128), exchange(after(part, right1), "dp", CHIPS))
    right3, left2 = rightward(after(right2, part)), leftward(after(left1, part))
    part = local(add_spread_kernel, shape(MP, R, 128), part, lax.ppermute(part, "dp", CORES))
    part = exchange(after(part, right2, left1), "mp")
    part = local(sum_spread_kernel, shape(DP // 2, R, 128), part)
    right4, left3 = rightward(after(right3, part)), leftward(after(left2, part))
    part = exchange(after(part, right3, left2), "dp", CHIPS)
    blocks = (tokens, right1, left1, right2, left2, right3, left3)
    p_factor, value, projected, rows, grads, near = local(
        right_kernel,
        (
            pltpu.VMEM((R, depth), F32),
            pltpu.VMEM((R, columns), F32),
            pltpu.VMEM((R, TOKENS), F32),
            pltpu.VMEM((TOKENS, depth), BF16),
            pltpu.VMEM((TOKENS, columns), BF16),
            pltpu.VMEM((depth, columns), BF16),
        ),
        part,
        far(err),
        far(out_grad),
        *blocks,
        spaces=[VMEM, hbm, hbm] + [pl.ANY] * 7,
        scratch=[dma((9,))],
    )
    p, grads, near = kept(p_factor), kept(grads), kept(near)
    mine, rows = local(
        right_last_kernel,
        (shape(R, columns), pltpu.VMEM((TOKENS, depth), BF16)),
        p,
        kept(value),
        kept(projected),
        grads,
        right4,
        kept(rows),
        scratch=[pltpu.VMEM((R, TOKENS), F32), dma],
        input_output_aliases={5: 1},
    )
    rows = kept(rows)
    out = (pltpu.VMEM((CHUNK, columns), F32), pltpu.VMEM((CHUNK, 6 * R), BF16))
    merged, lefts = zip(*[local(functools.partial(merged_kernel, i), out, p, rows, grads, near, mib=20) for i in range(depth // CHUNK)])
    for base, beside in ((2, merged[:1]), (8, merged[1:])):
        one, other, across = (lax.ppermute(mine, "dp", along(base, 4, step)) for step in (1, 3, 2))
        mine = local(add4_kernel, shape(R, columns), after(mine, *beside), across, one, other)
    other = lax.ppermute(mine, "dp", CORES)
    new_error, q_factor = pl.pallas_call(
        residue_kernel,
        out_shape=(shape(depth, columns, dtype=BF16), shape(R, columns)),
        in_specs=[pl.BlockSpec(memory_space=VMEM)] * (2 + 2 * len(merged)),
        out_specs=(pl.BlockSpec(memory_space=hbm), pl.BlockSpec(memory_space=VMEM)),
        scratch_shapes=[pltpu.VMEM((depth // PIECE, PIECE, columns), BF16), dma((depth // PIECE,))],
        compiler_params=pltpu.CompilerParams(vmem_limit_bytes=12 << 20),
    )(mine, other, *[kept(part) for part in merged + lefts])
    return (p_factor, q_factor, new_error[None])


def solution(mesh):
    placed = (P(("dp", "mp"), None), P("dp", "mp"), P("dp", None, "mp"), P(None, "mp"))
    return jax.shard_map(
        on_device,
        mesh=mesh,
        in_specs=placed,
        out_specs=(P(), P(None, "mp"), P("dp", None, "mp")),
        check_vma=False,
    )
```

```python
import functools

import jax
import jax.numpy as jnp
from jax import lax
from jax.experimental import pallas as pl
from jax.experimental.pallas import tpu as pltpu
from jax.sharding import PartitionSpec as P

MP = 8
DP = 32
R = 8
TOKENS = 1024
CHUNK = 512
F32 = jnp.float32
BF16 = jnp.bfloat16
VMEM = pltpu.MemorySpace.VMEM


def shift(size, step):
    return [(i, (i + step) % size) for i in range(size)]


CORES = [(i, i ^ 1) for i in range(DP)]
CHIPS = [[2 * i for i in range(DP // 2)], [2 * i + 1 for i in range(DP // 2)]]


def along(base, size, step):
    span = base * size
    return [(i, i // span * span + (i + base * step) % span) for i in range(DP)]


def after(x, *others):
    return lax.optimization_barrier((x,) + others)[0]


def terms(x):
    first = x.astype(BF16).astype(F32)
    rest = x - first
    second = rest.astype(BF16).astype(F32)
    return first, second, rest - second


def split3(x):
    return jnp.concatenate(terms(x), axis=0).astype(BF16)


def fold3(x):
    rows = x.shape[0] // 3
    return (x[2 * rows :] + x[rows : 2 * rows]) + x[:rows]


def dot(a, b, left, right):
    return lax.dot_general(a, b, (((left,), (right,)), ((), ())), preferred_element_type=F32)


def local(kernel, out, *args, spaces=None, mib=8, scratch=(), **kw):
    spaces = spaces or [VMEM] * len(args)
    return pl.pallas_call(
        kernel,
        out_shape=out,
        in_specs=[pl.BlockSpec(memory_space=s) for s in spaces],
        out_specs=jax.tree.map(lambda _: pl.BlockSpec(memory_space=VMEM), out),
        scratch_shapes=scratch,
        compiler_params=pltpu.CompilerParams(vmem_limit_bytes=mib << 20),
        **kw,
    )(*args)


def shape(*dims, dtype=F32):
    return jax.ShapeDtypeStruct(dims, dtype)


def pieces(size, count):
    step = size // count
    return [slice(i * step, (i + 1) * step) for i in range(count)]


def kept(x):
    return pltpu.with_memory_space_constraint(x, VMEM)


def far(x):
    return pltpu.with_memory_space_constraint(x, pltpu.MemorySpace.HBM)


def reduce_kernel(q_ref, g_ref, out_ref, q_held, held, sems):
    first = pltpu.make_async_copy(q_ref, q_held, sems.at[0])
    first.start()
    parts = pieces(TOKENS, 2)
    copies = [pltpu.make_async_copy(g_ref.at[at], held.at[at], sems.at[1 + i]) for i, at in enumerate(parts)]
    for copy in copies:
        copy.start()
    first.wait()
    q = split3(q_held[...])
    for i, (copy, at) in enumerate(zip(copies, parts)):
        copy.wait()
        value = fold3(dot(q, held[at], 1, 1))
        for j in range(4):
            out_ref[4 * i + j] = value[:, j * 128 : (j + 1) * 128]


def error_left_kernel(q_ref, err_ref, out_ref, q_held, held, sems):
    depth = err_ref.shape[0]
    first = pltpu.make_async_copy(q_ref, q_held, sems.at[0])
    first.start()
    copies = [pltpu.make_async_copy(err_ref.at[at], held.at[at], sems.at[1 + i]) for i, at in enumerate(pieces(depth, 4))]
    for copy in copies:
        copy.start()
    first.wait()
    q = split3(q_held[...])
    for copy, at in zip(copies, pieces(depth, 4)):
        copy.wait()
        out_ref[:, at] = fold3(dot(q, held[at], 1, 1))


def left_kernel(parts_ref, x_ref, more_ref, out_ref):
    reduced = jnp.sum(parts_ref[...], axis=0)
    value = fold3(dot(split3(reduced), x_ref[...], 1, 0)) + more_ref[...]
    for i in range(out_ref.shape[0]):
        out_ref[i] = value[:, i * 128 : (i + 1) * 128]


def sum_kernel(parts_ref, out_ref):
    out_ref[...] = jnp.sum(parts_ref[...], axis=0)


def add_spread_kernel(a_ref, b_ref, out_ref):
    out_ref[...] = jnp.broadcast_to((a_ref[...] + b_ref[...])[None], out_ref.shape)


def sum_spread_kernel(parts_ref, out_ref):
    value = jnp.sum(parts_ref[...], axis=0)
    out_ref[...] = jnp.broadcast_to(value[None], out_ref.shape)


def gram_schmidt(rows):
    index = lax.broadcasted_iota(jnp.int32, (R, 1), 0)
    for i in range(R):
        vector = rows[i : i + 1]
        products = jnp.sum(rows * vector, axis=1, keepdims=True)
        scale = 1.0 / jnp.sqrt(products[i : i + 1] + 1e-06)
        vector = vector * scale
        rows = jnp.where(index > i, rows - (products * scale) * vector, jnp.where(index == i, vector, rows))
    return rows


def starts_of():
    me = lax.axis_index("mp")
    owners = [me]
    for step in range(1, 4):
        owners += [lax.rem(me + MP - step, MP), lax.rem(me + step, MP)]
    owners.append(lax.rem(me + 4, MP))
    return [pl.multiple_of(owner * 128, 128) for owner in owners]


def right_kernel(parts_ref, err_ref, g_ref, *refs):
    blocks, (p_ref, value_ref, projected_ref, rows_ref, grads_ref, held_ref, sems) = refs[:7], refs[7:]
    copies = []
    for i, (block, start) in enumerate(zip(blocks, starts_of())):
        copies.append(pltpu.make_async_copy(block, rows_ref.at[pl.ds(start, 128)], sems.at[i]))
    copies.append(pltpu.make_async_copy(err_ref, held_ref, sems.at[7]))
    copies.append(pltpu.make_async_copy(g_ref, grads_ref, sems.at[8]))
    for copy in copies:
        copy.start()
    rows_ref[pl.ds(starts_of()[7], 128)] = jnp.zeros((128, rows_ref.shape[1]), BF16)
    p = gram_schmidt(jnp.concatenate([parts_ref[i] for i in range(parts_ref.shape[0])], axis=1))
    p_ref[...] = p
    left = split3(p)
    for block, start in zip(blocks, starts_of()):
        projected_ref[:, pl.ds(start, 128)] = fold3(dot(left, block[...], 1, 1))
    copies[7].wait()
    value_ref[...] = fold3(dot(left, held_ref[...], 1, 0))
    for copy in copies[:7] + copies[8:]:
        copy.wait()


def right_last_kernel(p_ref, value_ref, projected_ref, grads_ref, block_ref, old_ref, out_ref, rows_ref, total, sem):
    del old_ref
    start = starts_of()[7]
    copy = pltpu.make_async_copy(block_ref, rows_ref.at[pl.ds(start, 128)], sem)
    copy.start()
    total[...] = projected_ref[...]
    total[:, pl.ds(start, 128)] = fold3(dot(split3(p_ref[...]), block_ref[...], 1, 1))
    out_ref[...] = value_ref[...] + fold3(dot(split3(total[...]), grads_ref[...], 1, 0))
    copy.wait()


def merged_kernel(part, p_ref, rows_ref, grads_ref, err_ref, out_ref, left_ref):
    at = pl.ds(part * CHUNK, CHUNK)
    a, b, c = terms(p_ref[:, at])
    left_ref[...] = jnp.concatenate([a, a, a, b, b, c], axis=0).T.astype(BF16)
    out_ref[...] = dot(rows_ref[:, at], grads_ref[...], 0, 0) + err_ref[at].astype(F32)


def add4_kernel(own_ref, across_ref, one_ref, other_ref, out_ref):
    out_ref[...] = (own_ref[...] + across_ref[...]) + (one_ref[...] + other_ref[...])


def residue_kernel(mine_ref, other_ref, *refs):
    merged, lefts, (out_ref, q_ref, held, sems) = refs[:4], refs[4:8], refs[8:]
    q = (mine_ref[...] + other_ref[...]) / DP
    q_ref[...] = q
    a, b, c = terms(q)
    right = jnp.concatenate([a, b, c, a, b, a], axis=0).astype(BF16)
    copies = []
    for i, (part, left) in enumerate(zip(merged, lefts)):
        at = pl.ds(i * CHUNK, CHUNK)
        held[i] = (part[...] - dot(left[...], right, 1, 0)).astype(BF16)
        copies.append(pltpu.make_async_copy(held.at[i], out_ref.at[at], sems.at[i]))
        copies[-1].start()
    for copy in copies:
        copy.wait()


def exchange(x, axis, groups=None):
    return lax.all_to_all(x, axis, 0, 0, axis_index_groups=groups)


def on_device(tokens, out_grad, error, q_prev):
    err = error[0]
    depth, columns = err.shape

    def rightward(x):
        return lax.ppermute(x, "mp", shift(MP, 1))

    def leftward(x):
        return lax.ppermute(x, "mp", shift(MP, -1))

    right1 = rightward(tokens)
    hbm = pltpu.MemorySpace.HBM
    dma = pltpu.SemaphoreType.DMA
    held = pltpu.VMEM((R, columns), F32)
    reduced = local(
        reduce_kernel, shape(MP, R, 128), far(q_prev), far(out_grad), spaces=[hbm, hbm], scratch=[held, pltpu.VMEM(out_grad.shape, BF16), dma((5,))]
    )
    left1 = leftward(after(tokens, reduced))
    more = local(
        error_left_kernel, shape(R, depth), far(q_prev), far(err), spaces=[hbm, hbm], scratch=[held, pltpu.VMEM(err.shape, BF16), dma((5,))]
    )
    reduced = exchange(reduced, "mp")
    part = local(left_kernel, shape(DP // 2, R, 128), reduced, tokens, more)
    right2 = rightward(after(right1, part))
    part = local(sum_kernel, shape(R, 128), exchange(after(part, right1), "dp", CHIPS))
    right3, left2 = rightward(after(right2, part)), leftward(after(left1, part))
    part = local(add_spread_kernel, shape(MP, R, 128), part, lax.ppermute(part, "dp", CORES))
    part = exchange(after(part, right2, left1), "mp")
    part = local(sum_spread_kernel, shape(DP // 2, R, 128), part)
    right4, left3 = rightward(after(right3, part)), leftward(after(left2, part))
    part = exchange(after(part, right3, left2), "dp", CHIPS)
    blocks = (tokens, right1, left1, right2, left2, right3, left3)
    p_factor, value, projected, rows, grads, near = local(
        right_kernel,
        (
            pltpu.VMEM((R, depth), F32),
            pltpu.VMEM((R, columns), F32),
            pltpu.VMEM((R, TOKENS), F32),
            pltpu.VMEM((TOKENS, depth), BF16),
            pltpu.VMEM((TOKENS, columns), BF16),
            pltpu.VMEM((depth, columns), BF16),
        ),
        part,
        far(err),
        far(out_grad),
        *blocks,
        spaces=[VMEM, hbm, hbm] + [VMEM] * 7,
        scratch=[dma((9,))],
    )
    p, grads, near = kept(p_factor), kept(grads), kept(near)
    mine, rows = local(
        right_last_kernel,
        (shape(R, columns), pltpu.VMEM((TOKENS, depth), BF16)),
        p,
        kept(value),
        kept(projected),
        grads,
        right4,
        kept(rows),
        scratch=[pltpu.VMEM((R, TOKENS), F32), dma],
        input_output_aliases={5: 1},
    )
    rows = kept(rows)
    out = (pltpu.VMEM((CHUNK, columns), F32), pltpu.VMEM((CHUNK, 6 * R), BF16))
    merged, lefts = zip(*[local(functools.partial(merged_kernel, i), out, p, rows, grads, near) for i in range(depth // CHUNK)])
    for base, beside in ((2, merged[:2]), (8, merged[2:])):
        one, other, across = (lax.ppermute(mine, "dp", along(base, 4, step)) for step in (1, 3, 2))
        mine = local(add4_kernel, shape(R, columns), after(mine, *beside), across, one, other)
    other = lax.ppermute(mine, "dp", CORES)
    new_error, q_factor = pl.pallas_call(
        residue_kernel,
        out_shape=(shape(depth, columns, dtype=BF16), shape(R, columns)),
        in_specs=[pl.BlockSpec(memory_space=VMEM)] * (2 + 2 * len(merged)),
        out_specs=(pl.BlockSpec(memory_space=hbm), pl.BlockSpec(memory_space=VMEM)),
        scratch_shapes=[pltpu.VMEM((len(merged), CHUNK, columns), BF16), dma((len(merged),))],
        compiler_params=pltpu.CompilerParams(vmem_limit_bytes=12 << 20),
    )(mine, other, *[kept(part) for part in merged + lefts])
    return (p_factor, q_factor, new_error[None])


def solution(mesh):
    placed = (P(("dp", "mp"), None), P("dp", "mp"), P("dp", None, "mp"), P(None, "mp"))
    return jax.shard_map(
        on_device,
        mesh=mesh,
        in_specs=placed,
        out_specs=(P(), P(None, "mp"), P("dp", None, "mp")),
        check_vma=False,
    )
```
